32 devices in a mesh: parts: 2 (over x), outer: 2 (over core), inner: 8 (over z, y).
Axes of the slice: x: 2, y: 2, z: 4, core: 2. Of those that a mesh axis runs over, the one named last changes fastest.
Arguments:
- tokens: bfloat16 [2048, 3584], P(('parts', 'outer', 'inner')), parts along dimension 0, may hold values from -6 to 6
- scales: bfloat16 [2048, 28], P(('parts', 'outer', 'inner')), parts along dimension 0, may hold values from 0.5 to 2
- expert_ids: int32 [2048, 8], P(('parts', 'outer', 'inner')), parts along dimension 0, may hold values from 0 to 15, all different within a row; in each aligned block of 64 rows (0 to 63, 64 to 127, ...) at most 64 rows name the same one
- route_weights: float32 [2048, 8], P(('parts', 'outer', 'inner')), parts along dimension 0, may hold values from 0.05 to 0.5
- w_gate: bfloat16 [16, 3584, 1024], P(('outer', 'inner')), may hold values from -0.09375 to 0.09375
- w_up: bfloat16 [16, 3584, 1024], P(('outer', 'inner')), may hold values from -0.09375 to 0.09375
- w_down: bfloat16 [16, 1024, 3584], P(('outer', 'inner')), may hold values from -0.1875 to 0.1875
Outputs:
- mixed: bfloat16 [2048, 3584], P(('parts', 'outer', 'inner')), parts along dimension 0
The draws below stay inside these ranges and needn't reach their ends.
There are 2 independent parts, one for each index of `parts`. The reference program is written for one: setup_inputs(seed, part) draws one part's arguments, and reference() takes and returns one part's arrays. A program takes and returns all parts, laid end to end along the dimension named above; an argument that names none is the same for every part. Nothing has to cross between parts.
Inputs may be any that keep to these rules, and one draw needn't show every extreme that they name: `expert_ids`: each row names 8 different experts; among the rows of one device no expert is named more than 64 times.
All inputs are finite; a program needn't handle non-finite values.
Results may differ from the reference program's by a relative error of at most 0.0071.
Values may be sent and summed in bfloat16 or wider, within the bound.
A program may use at most 128 MiB of HBM per device.

```python
import math
import jax
import jax.numpy as jnp
import numpy as np
from jax import lax

D = 3584
FF = 1024
TOP = 8
TOK_DEV = 64
EXPERTS = 16
CAP_SRC = 64
TOKENS = 1024


def level_of(key, extent, split, smallest, high):
    factor_of, own = 1.0, jax.random.fold_in(key, 6)
    for axis_at, blocks in split:
        heights = jnp.exp(jax.random.uniform(jax.random.fold_in(own, axis_at), (blocks,), jnp.float32, smallest / len(split), high / len(split)))
        factor_of = factor_of * jnp.repeat(heights, extent[axis_at] // blocks).reshape([-1 if axis == axis_at else 1 for axis in range(len(extent))])
    return factor_of


def shared_out(key, own, number, rows, number_of, top, reach, slope):
    sequence = jax.random.permutation(key, number_of)
    packed, common = load_shares(number_of, rows * top, reach, slope, True), load_shares(number_of, rows * top, reach, slope, False)
    places = jnp.arange(number_of)

    def named(lengths, turn):
        used = int((lengths > 0).sum())
        fixed = max(1, used // 4)
        shifted = fixed + (places - fixed + turn * (used - fixed)) % max(1, number_of - fixed)
        return jnp.zeros((number_of,), jnp.int32).at[sequence[jnp.where(places < fixed, places, shifted)]].set(jnp.asarray(lengths, jnp.int32))

    lengths = jnp.where(number % 4 == 0, named(packed, number // 4), named(common, number - number // 4 - 1))
    mixed = jax.random.permutation(jax.random.fold_in(own, 3), number_of)
    giver, taker = mixed[0:number_of // 2 * 2:2], mixed[1:number_of // 2 * 2:2]
    margin = jnp.minimum(lengths[giver] - 1, reach - lengths[taker]) // 2
    margin = jnp.where((giver == sequence[0]) | (taker == sequence[0]) | (lengths[taker] == 0), 0, jnp.maximum(margin, 0))
    shifted = jax.random.randint(jax.random.fold_in(own, 4), (number_of // 2,), 0, 1 << 20) % (margin + 1)
    lengths = lengths.at[giver].add(-shifted).at[taker].add(shifted)
    members = jnp.searchsorted(jnp.cumsum(lengths), jnp.arange(rows * top), side="right").astype(jnp.int32)
    grid = members.reshape(top, rows).T
    grid = grid[jax.random.permutation(jax.random.fold_in(own, 1), rows)]
    turn = jax.random.randint(jax.random.fold_in(own, 2), (rows, 1), 0, top)
    return jnp.take_along_axis(grid, (jnp.arange(top)[None, :] + turn) % top, axis=1)


def load_shares(count, total, reach, lean, full):
    weights = [(1 << 20) // math.isqrt(rank ** lean) + 1 for rank in range(1, count + 1)]
    largest = reach if full else min(reach, max(-(-total // count), total * weights[0] // sum(weights)))
    least = 1 if total - largest >= count - 1 else 0
    counts, rest = [largest] + [least] * (count - 1), total - largest - least * (count - 1)
    while rest > 0:
        movable = [i for i in range(1, count) if counts[i] < largest] or [i for i in range(1, count) if counts[i] < reach]
        whole, remaining = sum([weights[i] for i in movable]), rest
        for i in movable:
            addition = min(reach - counts[i], max(1, remaining * weights[i] // whole), rest)
            counts[i] = counts[i] + addition
            rest = rest - addition
    return np.array(counts)


def noise(key, extent, width, limit, shards=(), kind=jnp.bfloat16):
    loudness = level_of(key, extent, shards, -0.22, 0.18) if shards else 1.0
    entries = jax.random.normal(key, extent, jnp.float32) * width * loudness
    return jnp.minimum(jnp.maximum(entries, -limit), limit).astype(kind)


def setup_inputs(seed: int = 0, part: int = 0) -> dict:
    arg_keys = jax.random.split(jax.random.key(seed), 8)
    part_keys = jax.random.split(jax.random.fold_in(arg_keys[7], part), 8)
    tokens = noise(part_keys[0], (TOKENS, D), 1.0, 6.0, ((0, 16),))
    scales = jnp.clip(jnp.exp(math.log(2.0) - 1.3862944 * jax.random.uniform(part_keys[1], (TOKENS, D // 128), jnp.float32) ** level_of(part_keys[1], (TOKENS, D // 128), ((0, 16),), -0.2, 0.2)), 0.5, 2.0).astype(jnp.bfloat16)
    expert_ids_keys = jax.random.split(jax.random.fold_in(part_keys[2], 1), TOKENS // TOK_DEV)
    expert_ids_turns = jax.random.permutation(jax.random.fold_in(part_keys[2], 3), TOKENS // TOK_DEV)
    expert_ids = jax.vmap(lambda own, number: shared_out(jax.random.fold_in(part_keys[2], 2), own, number, TOK_DEV, EXPERTS, TOP, CAP_SRC, 1))(expert_ids_keys, expert_ids_turns).reshape((TOKENS, TOP))
    route_weights = jnp.clip(jnp.exp(math.log(0.5) - 2.3025851 * jax.random.uniform(part_keys[3], (TOKENS, TOP), jnp.float32) ** level_of(part_keys[3], (TOKENS, TOP), ((0, 16),), -0.2, 0.2)), 0.05, 0.5)
    w_gate = noise(arg_keys[4], (EXPERTS, D, FF), D ** -0.5, 0.09375, ((0, 16),))
    w_up = noise(arg_keys[5], (EXPERTS, D, FF), D ** -0.5, 0.09375, ((0, 16),))
    w_down = noise(arg_keys[6], (EXPERTS, FF, D), FF ** -0.5, 0.1875, ((0, 16),))
    return {"tokens": tokens, "scales": scales, "expert_ids": expert_ids, "route_weights": route_weights, "w_gate": w_gate, "w_up": w_up, "w_down": w_down}


def dequantize(values, block_scales):
    row_count, model_width = values.shape
    scaled = values.astype(jnp.float32).reshape(row_count, model_width // 128, 128) * block_scales.astype(jnp.float32)[:, :, None]
    return scaled.reshape(row_count, model_width).astype(jnp.bfloat16)


def expert_ffn(row_block, gate_weight, up_weight, down_weight):
    gate_proj = jnp.dot(row_block, gate_weight, preferred_element_type=jnp.float32)
    up_proj = jnp.dot(row_block, up_weight, preferred_element_type=jnp.float32)
    hidden = (jax.nn.silu(gate_proj) * up_proj).astype(jnp.bfloat16)
    return jnp.dot(hidden, down_weight, preferred_element_type=jnp.float32).astype(jnp.bfloat16)


def route_positions(flat_ids, expert_count):
    onehot = (flat_ids[:, :, None] == jnp.arange(expert_count, dtype=jnp.int32)[None, None, :]).astype(jnp.int32)
    before = jnp.cumsum(onehot, axis=1) - onehot
    return jnp.sum(before * onehot, axis=2).astype(jnp.int32)


def reference(tokens, scales, expert_ids, route_weights, w_gate, w_up, w_down):
    sources = TOKENS // TOK_DEV
    dequant = dequantize(tokens, scales)
    flat_ids = expert_ids.reshape(sources, TOK_DEV * TOP)
    position = route_positions(flat_ids, EXPERTS)
    source_index = jnp.arange(sources, dtype=jnp.int32)[:, None]
    slot_index = (flat_ids * (sources * CAP_SRC) + source_index * CAP_SRC + position).reshape(-1).astype(jnp.int32)
    route_rows = (jnp.arange(TOKENS * TOP, dtype=jnp.int32) // TOP).astype(jnp.int32)
    slot_table = jnp.full((EXPERTS * sources * CAP_SRC,), TOKENS, jnp.int32).at[slot_index].set(route_rows)
    padded = jnp.concatenate([dequant, jnp.zeros((1, D), jnp.bfloat16)], axis=0)

    def serve(expert_args):
        table_part, gate_weight, up_weight, down_weight = expert_args
        return expert_ffn(padded[table_part], gate_weight, up_weight, down_weight)

    outputs = lax.map(serve, (slot_table.reshape(EXPERTS, sources * CAP_SRC), w_gate, w_up, w_down))
    collected = outputs.reshape(EXPERTS * sources * CAP_SRC, D)[slot_index].astype(jnp.float32).reshape(TOKENS, TOP, D)
    return jnp.sum(collected * route_weights[:, :, None], axis=1).astype(jnp.bfloat16)
```

```python
import jax
import jax.numpy as jnp
from jax import lax
from jax.sharding import PartitionSpec as P

GROUP = ("outer", "inner")


def dequantize(values, block_scales):
    row_count, model_width = values.shape
    scaled = (
        values.astype(jnp.float32).reshape(row_count, model_width // 128, 128)
        * block_scales.astype(jnp.float32)[:, :, None]
    )
    return scaled.reshape(row_count, model_width).astype(jnp.bfloat16)


def body(tokens, scales, expert_ids, route_weights, w_gate, w_up, w_down):
    groups = lax.axis_size("outer") * lax.axis_size("inner")
    me = lax.axis_index("outer") * lax.axis_size("inner") + lax.axis_index("inner")
    experts = jnp.arange(groups, dtype=jnp.int32)
    dense = jnp.sum(
        jnp.where(expert_ids[:, :, None] == experts, route_weights[:, :, None], 0.0), axis=1
    )
    mine = lax.all_gather(dense, GROUP, axis=0, tiled=True)
    weight = lax.dynamic_slice_in_dim(mine, me, 1, axis=1)
    rows = lax.all_gather(dequantize(tokens, scales), GROUP, axis=0, tiled=True)
    gate = jnp.dot(rows, w_gate[0], preferred_element_type=jnp.float32)
    up = jnp.dot(rows, w_up[0], preferred_element_type=jnp.float32)
    hidden = (jax.nn.silu(gate) * up).astype(jnp.bfloat16)
    out = jnp.dot(hidden, w_down[0], preferred_element_type=jnp.float32)
    out = (out * weight).astype(jnp.bfloat16)
    return lax.psum_scatter(out, GROUP, scatter_dimension=0, tiled=True)


def solution(mesh):
    rows = P(("parts", "outer", "inner"), None)
    weights = P(("outer", "inner"), None, None)
    return jax.shard_map(
        body,
        mesh=mesh,
        in_specs=(rows, rows, rows, rows, weights, weights, weights),
        out_specs=rows,
        check_vma=False,
    )
```

```python
import functools

import jax
import jax.numpy as jnp
from jax import lax
from jax.experimental import pallas as pl
from jax.experimental.pallas import tpu as pltpu
from jax.sharding import PartitionSpec as P

LANES = 128
TILE = 256
MESH = pl.DeviceIdType.MESH


def ring_position(chips, index):
    if chips > 8:
        return index
    z, y = index // 2, index % 2
    return z + y * (chips - 1 - 2 * z)


def ring_index(chips, position):
    if chips > 8:
        return position
    back = position // (chips // 2)
    return (1 - back) * 2 * position + back * (2 * (chips - 1 - position) + 1)


def kernel(
    chips, experts,
    tokens, scales, ids, weights, gate_hbm, up_hbm, down_hbm,
    out,
    wg, wu, wd, rows, hidden, own, first, part_out, part_in, sums,
    w_sem, tok_send, tok_recv, swap_send, swap_recv, part_send, part_recv, sum_send, sum_recv,
):
    core = lax.axis_index("outer")
    index = lax.axis_index("inner")
    me = core * chips + index
    position = ring_position(chips, index)
    right = {"inner": ring_index(chips, (position + 1) % chips)}
    left = {"inner": ring_index(chips, (position + chips - 1) % chips)}
    twin = {"outer": 1 - core}
    count, width = tokens.shape
    half = count // 2
    tiles = width // TILE
    ways = ((0, right), (1, left))

    loads = [
        pltpu.make_async_copy(gate_hbm.at[0], wg, w_sem.at[0]),
        pltpu.make_async_copy(up_hbm.at[0], wu, w_sem.at[1]),
        pltpu.make_async_copy(down_hbm.at[0], wd, w_sem.at[2]),
    ]
    for load in loads:
        load.start()

    barrier = pltpu.get_barrier_semaphore()
    for other in (right, left, twin):
        pl.semaphore_signal(barrier, inc=1, device_id=other, device_id_type=MESH)

    for block in range(width // LANES):
        columns = slice(block * LANES, (block + 1) * LANES)
        scaled = tokens[:, columns].astype(jnp.float32) * scales[:, block:block + 1].astype(jnp.float32)
        rows[0, :count, columns] = scaled.astype(jnp.bfloat16)
    lane = lax.broadcasted_iota(jnp.int32, (count, LANES), 1)
    dense = jnp.zeros((count, LANES), jnp.float32)
    for route in range(ids.shape[1]):
        dense = dense + jnp.where(ids[:, route:route + 1] == lane % experts, weights[:, route:route + 1], 0.0)
    high = dense.astype(jnp.bfloat16).astype(jnp.float32)
    middle = (dense - high).astype(jnp.bfloat16).astype(jnp.float32)
    low = dense - high - middle
    piece = lane // experts
    packed = jnp.where(piece == 0, high, jnp.where(piece == 1, middle, jnp.where(piece == 2, low, 0.0)))
    rows[0, :count, width:] = packed.astype(jnp.bfloat16)
    sums[0] = jnp.zeros((count, width), jnp.bfloat16)

    def token_copy(step, way, target):
        part = pl.ds(way * half, half)
        return pltpu.make_async_remote_copy(
            src_ref=rows.at[step, part], dst_ref=rows.at[step + 1, part],
            send_sem=tok_send.at[step, way], recv_sem=tok_recv.at[step + 1, way],
            device_id=target, device_id_type=MESH,
        )

    def swap_copy(step):
        return pltpu.make_async_remote_copy(
            src_ref=rows.at[step, pl.ds(0, count)], dst_ref=rows.at[step, pl.ds(count, count)],
            send_sem=swap_send.at[step], recv_sem=swap_recv.at[step],
            device_id=twin, device_id_type=MESH,
        )

    def part_copy(step):
        return pltpu.make_async_remote_copy(
            src_ref=part_out.at[step % 2], dst_ref=part_in.at[step],
            send_sem=part_send.at[step], recv_sem=part_recv.at[step],
            device_id=twin, device_id_type=MESH,
        )

    def sum_copy(step, way, target):
        part = pl.ds(way * half, half)
        return pltpu.make_async_remote_copy(
            src_ref=sums.at[step - 1, part], dst_ref=sums.at[step, part],
            send_sem=sum_send.at[step - 1, way], recv_sem=sum_recv.at[step, way],
            device_id=target, device_id_type=MESH,
        )

    def pass_on(step):
        @pl.when(step > 0)
        def _():
            for way, target in ways:
                token_copy(step - 1, way, target).wait_recv()

        @pl.when(step < chips - 1)
        def _():
            for way, target in ways:
                token_copy(step, way, target).start()

        swap_copy(step).start()

    def ffn(step):
        def up_tile(tile, carry):
            columns = pl.ds(pl.multiple_of(tile * TILE, TILE), TILE)
            block = rows[step, :, :width]
            gate = jnp.dot(block, wg[:, columns], preferred_element_type=jnp.float32)
            up = jnp.dot(block, wu[:, columns], preferred_element_type=jnp.float32)
            hidden[:, columns] = (gate / (1.0 + jnp.exp(-gate)) * up).astype(jnp.bfloat16)
            return carry

        lax.fori_loop(0, hidden.shape[1] // TILE, up_tile, 0)
        lane = lax.broadcasted_iota(jnp.int32, (2 * count, LANES), 1)
        packed = rows[step, :, width:].astype(jnp.float32)
        share = jnp.sum(jnp.where(lane % experts == me, packed, 0.0), axis=1, keepdims=True)

        def down_tile(tile, carry):
            columns = pl.ds(pl.multiple_of(tile * TILE, TILE), TILE)
            result = jnp.dot(hidden[...], wd[:, columns], preferred_element_type=jnp.float32) * share
            own[:, columns] = result[:count]
            part_out[step % 2, :, columns] = result[count:].astype(jnp.bfloat16)
            return carry

        lax.fori_loop(0, tiles, down_tile, 0)

    pl.semaphore_wait(barrier, 3)
    pass_on(0)
    swap_copy(0).wait_recv()
    for load in loads:
        load.wait()
    ffn(0)
    part_copy(0).start()
    pass_on(1)
    part_copy(0).wait_recv()

    def keep_tile(tile, carry):
        columns = pl.ds(pl.multiple_of(tile * TILE, TILE), TILE)
        first[:, columns] = own[:, columns] + part_in[0, :, columns].astype(jnp.float32)
        return carry

    lax.fori_loop(0, tiles, keep_tile, 0)

    def send_sums(step):
        part_copy(step).wait_recv()

        @pl.when(step > 1)
        def _():
            for way, target in ways:
                sum_copy(step - 1, way, target).wait_recv()

        def add_tile(tile, carry):
            columns = pl.ds(pl.multiple_of(tile * TILE, TILE), TILE)
            total = own[:, columns] + part_in[step, :, columns].astype(jnp.float32)
            total = total + sums[step - 1, :, columns].astype(jnp.float32)
            sums[step - 1, :, columns] = total.astype(jnp.bfloat16)
            return carry

        lax.fori_loop(0, tiles, add_tile, 0)
        for way, target in ways:
            sum_copy(step, way, target).start()

    def turn(step, carry):
        swap_copy(step).wait_recv()

        @pl.when(step > 1)
        def _():
            part_copy(step - 2).wait_send()

        ffn(step)
        part_copy(step).start()

        @pl.when(step < chips - 1)
        def _():
            pass_on(step + 1)

        send_sums(step)
        return carry

    lax.fori_loop(1, chips, turn, 0)
    for way, target in ways:
        sum_copy(chips - 1, way, target).wait_recv()

    def last_tile(tile, carry):
        columns = pl.ds(pl.multiple_of(tile * TILE, TILE), TILE)
        total = first[:, columns] + sums[chips - 1, :, columns].astype(jnp.float32)
        out[:, columns] = total.astype(jnp.bfloat16)
        return carry

    lax.fori_loop(0, tiles, last_tile, 0)
    part_copy(chips - 1).wait_send()
    part_copy(chips - 2).wait_send()

    def drain(step, carry):
        for way, target in ways:
            token_copy(step, way, target).wait_send()
            sum_copy(step + 1, way, target).wait_send()
        return carry

    lax.fori_loop(0, chips - 1, drain, 0)

    def drain_swaps(step, carry):
        swap_copy(step).wait_send()
        return carry

    lax.fori_loop(0, chips, drain_swaps, 0)


def body(tokens, scales, expert_ids, route_weights, w_gate, w_up, w_down):
    chips = lax.axis_size("inner")
    experts = lax.axis_size("outer") * chips
    count, width = tokens.shape
    ff = w_gate.shape[2]
    vmem = pl.BlockSpec(memory_space=pltpu.VMEM)
    hbm = pl.BlockSpec(memory_space=pl.ANY)
    dma = pltpu.SemaphoreType.DMA
    flops = 12 * chips * count * width * ff
    return pl.pallas_call(
        functools.partial(kernel, chips, experts),
        out_shape=jax.ShapeDtypeStruct((count, width), jnp.bfloat16),
        in_specs=[vmem] * 4 + [hbm] * 3,
        out_specs=vmem,
        scratch_shapes=[
            pltpu.VMEM((width, ff), jnp.bfloat16),
            pltpu.VMEM((width, ff), jnp.bfloat16),
            pltpu.VMEM((ff, width), jnp.bfloat16),
            pltpu.VMEM((chips, 2 * count, width + LANES), jnp.bfloat16),
            pltpu.VMEM((2 * count, ff), jnp.bfloat16),
            pltpu.VMEM((count, width), jnp.float32),
            pltpu.VMEM((count, width), jnp.float32),
            pltpu.VMEM((2, count, width), jnp.bfloat16),
            pltpu.VMEM((chips, count, width), jnp.bfloat16),
            pltpu.VMEM((chips, count, width), jnp.bfloat16),
            dma((3,)),
            dma((chips, 2)), dma((chips, 2)),
            dma((chips,)), dma((chips,)),
            dma((chips,)), dma((chips,)),
            dma((chips, 2)), dma((chips, 2)),
        ],
        cost_estimate=pl.CostEstimate(
            flops=flops, bytes_accessed=6 * width * ff, transcendentals=2 * chips * count * ff
        ),
        compiler_params=pltpu.CompilerParams(
            collective_id=0, has_side_effects=True, vmem_limit_bytes=60 * 1024 * 1024
        ),
    )(tokens, scales, expert_ids, route_weights, w_gate, w_up, w_down)


def solution(mesh):
    rows = P(("parts", "outer", "inner"), None)
    weights = P(("outer", "inner"), None, None)
    return jax.shard_map(
        body,
        mesh=mesh,
        in_specs=(rows, rows, rows, rows, weights, weights, weights),
        out_specs=rows,
        check_vma=False,
    )
```

```python
import functools

import jax
import jax.numpy as jnp
from jax import lax
from jax.experimental import pallas as pl
from jax.experimental.pallas import tpu as pltpu
from jax.sharding import PartitionSpec as P

LANES = 128
TILE = 256
PIECES = 2
MESH = pl.DeviceIdType.MESH


def ring_position(chips, index):
    if chips > 8:
        return index
    z, y = index // 2, index % 2
    return z + y * (chips - 1 - 2 * z)


def ring_index(chips, position):
    if chips > 8:
        return position
    back = position // (chips // 2)
    return (1 - back) * 2 * position + back * (2 * (chips - 1 - position) + 1)


def kernel(
    chips, experts,
    tokens, scales, ids, weights, gate_hbm, up_hbm, down_hbm,
    out,
    wg, wu, wd, rows, hidden, own, first, part_out, part_in, sums,
    w_sem, tok_send, tok_recv, swap_send, swap_recv, part_send, part_recv, sum_send, sum_recv,
):
    core = lax.axis_index("outer")
    index = lax.axis_index("inner")
    me = core * chips + index
    position = ring_position(chips, index)
    right = {"inner": ring_index(chips, (position + 1) % chips)}
    left = {"inner": ring_index(chips, (position + chips - 1) % chips)}
    twin = {"outer": 1 - core}
    count, width = tokens.shape
    half = count // 2
    tiles = width // TILE
    chunk = width // PIECES
    ways = ((0, right), (1, left))

    loads = [
        pltpu.make_async_copy(gate_hbm.at[0], wg, w_sem.at[0]),
        pltpu.make_async_copy(up_hbm.at[0], wu, w_sem.at[1]),
        pltpu.make_async_copy(down_hbm.at[0], wd, w_sem.at[2]),
    ]
    for load in loads:
        load.start()

    barrier = pltpu.get_barrier_semaphore()
    for other in (right, left, twin):
        pl.semaphore_signal(barrier, inc=1, device_id=other, device_id_type=MESH)

    for block in range(width // LANES):
        columns = slice(block * LANES, (block + 1) * LANES)
        scaled = tokens[:, columns].astype(jnp.float32) * scales[:, block:block + 1].astype(jnp.float32)
        rows[0, :count, columns] = scaled.astype(jnp.bfloat16)
    lane = lax.broadcasted_iota(jnp.int32, (count, LANES), 1)
    dense = jnp.zeros((count, LANES), jnp.float32)
    for route in range(ids.shape[1]):
        dense = dense + jnp.where(ids[:, route:route + 1] == lane % experts, weights[:, route:route + 1], 0.0)
    high = dense.astype(jnp.bfloat16).astype(jnp.float32)
    middle = (dense - high).astype(jnp.bfloat16).astype(jnp.float32)
    low = dense - high - middle
    piece = lane // experts
    packed = jnp.where(piece == 0, high, jnp.where(piece == 1, middle, jnp.where(piece == 2, low, 0.0)))
    rows[0, :count, width:] = packed.astype(jnp.bfloat16)
    sums[0] = jnp.zeros((count, width), jnp.bfloat16)

    def token_copy(step, way, piece, target):
        size = chunk if piece < PIECES - 1 else chunk + LANES
        part = (pl.ds(way * half, half), pl.ds(piece * chunk, size))
        return pltpu.make_async_remote_copy(
            src_ref=rows.at[step, *part], dst_ref=rows.at[step + 1, *part],
            send_sem=tok_send.at[step, way, piece], recv_sem=tok_recv.at[step + 1, way, piece],
            device_id=target, device_id_type=MESH,
        )

    def swap_copy(step):
        return pltpu.make_async_remote_copy(
            src_ref=rows.at[step, pl.ds(0, count)], dst_ref=rows.at[step, pl.ds(count, count)],
            send_sem=swap_send.at[step], recv_sem=swap_recv.at[step],
            device_id=twin, device_id_type=MESH,
        )

    def part_copy(step):
        return pltpu.make_async_remote_copy(
            src_ref=part_out.at[step % 2], dst_ref=part_in.at[step],
            send_sem=part_send.at[step], recv_sem=part_recv.at[step],
            device_id=twin, device_id_type=MESH,
        )

    def sum_copy(step, way, piece, target):
        part = (pl.ds(way * half, half), pl.ds(piece * chunk, chunk))
        return pltpu.make_async_remote_copy(
            src_ref=sums.at[step - 1, *part], dst_ref=sums.at[step, *part],
            send_sem=sum_send.at[step - 1, way, piece], recv_sem=sum_recv.at[step, way, piece],
            device_id=target, device_id_type=MESH,
        )

    def pass_on(step):
        for piece in range(PIECES):
            @pl.when(step > 0)
            def _():
                for way, target in ways:
                    token_copy(step - 1, way, piece, target).wait_recv()

            @pl.when(step < chips - 1)
            def _():
                for way, target in ways:
                    token_copy(step, way, piece, target).start()

        swap_copy(step).start()

    def up_phase(pair):
        def up_tile(tile, carry):
            columns = pl.ds(pl.multiple_of(tile * TILE, TILE), TILE)
            block = rows[pl.ds(2 * pair, 2), :, :width].reshape(4 * count, width)
            gate = jnp.dot(block, wg[:, columns], preferred_element_type=jnp.float32)
            up = jnp.dot(block, wu[:, columns], preferred_element_type=jnp.float32)
            hidden[:, columns] = (gate / (1.0 + jnp.exp(-gate)) * up).astype(jnp.bfloat16)
            return carry

        lax.fori_loop(0, hidden.shape[1] // TILE, up_tile, 0)

    def down_phase(pair):
        lane = lax.broadcasted_iota(jnp.int32, (4 * count, LANES), 1)
        packed = rows[pl.ds(2 * pair, 2), :, width:].reshape(4 * count, LANES).astype(jnp.float32)
        share = jnp.sum(jnp.where(lane % experts == me, packed, 0.0), axis=1, keepdims=True)

        def down_tile(tile, carry):
            columns = pl.ds(pl.multiple_of(tile * TILE, TILE), TILE)
            result = jnp.dot(hidden[...], wd[:, columns], preferred_element_type=jnp.float32) * share
            for turn in range(2):
                at = 2 * turn * count
                own[turn, :, columns] = result[at:at + count]
                part_out[turn, :, columns] = result[at + count:at + 2 * count].astype(jnp.bfloat16)
            return carry

        lax.fori_loop(0, tiles, down_tile, 0)

    pl.semaphore_wait(barrier, 3)
    pass_on(0)
    pass_on(1)
    loads[0].wait()
    loads[1].wait()

    def keep_first():
        part_copy(0).wait_recv()

        def keep_tile(tile, carry):
            columns = pl.ds(pl.multiple_of(tile * TILE, TILE), TILE)
            first[:, columns] = own[0, :, columns] + part_in[0, :, columns].astype(jnp.float32)
            return carry

        lax.fori_loop(0, tiles, keep_tile, 0)

    def send_sums(step):
        part_copy(step).wait_recv()

        for piece in range(PIECES):
            @pl.when(step > 1)
            def _():
                for way, target in ways:
                    sum_copy(step - 1, way, piece, target).wait_recv()

            def add_tile(tile, carry):
                columns = pl.ds(pl.multiple_of(piece * chunk + tile * TILE, TILE), TILE)
                total = own[step % 2, :, columns] + part_in[step, :, columns].astype(jnp.float32)
                total = total + sums[step - 1, :, columns].astype(jnp.float32)
                sums[step - 1, :, columns] = total.astype(jnp.bfloat16)
                return carry

            lax.fori_loop(0, chunk // TILE, add_tile, 0)
            for way, target in ways:
                sum_copy(step, way, piece, target).start()

    def turn(pair, carry):
        swap_copy(2 * pair).wait_recv()
        swap_copy(2 * pair + 1).wait_recv()
        up_phase(pair)

        @pl.when(2 * pair + 2 < chips)
        def _():
            pass_on(2 * pair + 2)

        @pl.when(pair == 0)
        def _():
            loads[2].wait()

        @pl.when(pair > 1)
        def _():
            send_sums(2 * pair - 1)

        @pl.when(pair > 0)
        def _():
            part_copy(2 * pair - 2).wait_send()
            part_copy(2 * pair - 1).wait_send()

        down_phase(pair)
        part_copy(2 * pair).start()
        part_copy(2 * pair + 1).start()

        @pl.when(2 * pair + 3 < chips)
        def _():
            pass_on(2 * pair + 3)

        @pl.when(pair == 0)
        def _():
            send_sums(1)
            keep_first()

        @pl.when(pair > 0)
        def _():
            send_sums(2 * pair)

        return carry

    lax.fori_loop(0, chips // 2, turn, 0)
    send_sums(chips - 1)
    for piece in range(PIECES):
        for way, target in ways:
            sum_copy(chips - 1, way, piece, target).wait_recv()

        def last_tile(tile, carry):
            columns = pl.ds(pl.multiple_of(piece * chunk + tile * TILE, TILE), TILE)
            total = first[:, columns] + sums[chips - 1, :, columns].astype(jnp.float32)
            out[:, columns] = total.astype(jnp.bfloat16)
            return carry

        lax.fori_loop(0, chunk // TILE, last_tile, 0)

    part_copy(chips - 1).wait_send()
    part_copy(chips - 2).wait_send()

    def drain(step, carry):
        for way, target in ways:
            for piece in range(PIECES):
                token_copy(step, way, piece, target).wait_send()
                sum_copy(step + 1, way, piece, target).wait_send()
        return carry

    lax.fori_loop(0, chips - 1, drain, 0)

    def drain_swaps(step, carry):
        swap_copy(step).wait_send()
        return carry

    lax.fori_loop(0, chips, drain_swaps, 0)


def body(tokens, scales, expert_ids, route_weights, w_gate, w_up, w_down):
    chips = lax.axis_size("inner")
    experts = lax.axis_size("outer") * chips
    count, width = tokens.shape
    ff = w_gate.shape[2]
    vmem = pl.BlockSpec(memory_space=pltpu.VMEM)
    hbm = pl.BlockSpec(memory_space=pl.ANY)
    dma = pltpu.SemaphoreType.DMA
    flops = 12 * chips * count * width * ff
    return pl.pallas_call(
        functools.partial(kernel, chips, experts),
        out_shape=jax.ShapeDtypeStruct((count, width), jnp.bfloat16),
        in_specs=[vmem] * 4 + [hbm] * 3,
        out_specs=vmem,
        scratch_shapes=[
            pltpu.VMEM((width, ff), jnp.bfloat16),
            pltpu.VMEM((width, ff), jnp.bfloat16),
            pltpu.VMEM((ff, width), jnp.bfloat16),
            pltpu.VMEM((chips, 2 * count, width + LANES), jnp.bfloat16),
            pltpu.VMEM((4 * count, ff), jnp.bfloat16),
            pltpu.VMEM((2, count, width), jnp.float32),
            pltpu.VMEM((count, width), jnp.float32),
            pltpu.VMEM((2, count, width), jnp.bfloat16),
            pltpu.VMEM((chips, count, width), jnp.bfloat16),
            pltpu.VMEM((chips, count, width), jnp.bfloat16),
            dma((3,)),
            dma((chips, 2, PIECES)), dma((chips, 2, PIECES)),
            dma((chips,)), dma((chips,)),
            dma((chips,)), dma((chips,)),
            dma((chips, 2, PIECES)), dma((chips, 2, PIECES)),
        ],
        cost_estimate=pl.CostEstimate(
            flops=flops, bytes_accessed=6 * width * ff, transcendentals=2 * chips * count * ff
        ),
        compiler_params=pltpu.CompilerParams(
            collective_id=0, has_side_effects=True, vmem_limit_bytes=60 * 1024 * 1024
        ),
    )(tokens, scales, expert_ids, route_weights, w_gate, w_up, w_down)


def solution(mesh):
    rows = P(("parts", "outer", "inner"), None)
    weights = P(("outer", "inner"), None, None)
    return jax.shard_map(
        body,
        mesh=mesh,
        in_specs=(rows, rows, rows, rows, weights, weights, weights),
        out_specs=rows,
        check_vma=False,
    )
```

```python
import functools

import jax
import jax.numpy as jnp
from jax import lax
from jax.experimental import pallas as pl
from jax.experimental.pallas import tpu as pltpu
from jax.sharding import PartitionSpec as P

LANES = 128
TILE = 256
PIECES = 2
MESH = pl.DeviceIdType.MESH


def ring_position(chips, index):
    if chips > 8:
        return index
    z, y = index // 2, index % 2
    return z + y * (chips - 1 - 2 * z)


def ring_index(chips, position):
    if chips > 8:
        return position
    back = position // (chips // 2)
    return (1 - back) * 2 * position + back * (2 * (chips - 1 - position) + 1)


def kernel(
    chips, experts,
    tokens, scales, ids, weights, gate_hbm, up_hbm, down_hbm,
    out,
    wg, wu, wd, rows, hidden, own, first, part_out, part_in, sums,
    w_sem, tok_send, tok_recv, swap_send, swap_recv, part_send, part_recv, sum_send, sum_recv,
):
    core = lax.axis_index("outer")
    index = lax.axis_index("inner")
    me = core * chips + index
    position = ring_position(chips, index)
    right = {"inner": ring_index(chips, (position + 1) % chips)}
    left = {"inner": ring_index(chips, (position + chips - 1) % chips)}
    twin = {"outer": 1 - core}
    count, width = tokens.shape
    half = count // 2
    tiles = width // TILE
    chunk = width // PIECES
    ways = ((0, right), (1, left))

    loads = [
        pltpu.make_async_copy(gate_hbm.at[0], wg, w_sem.at[0]),
        pltpu.make_async_copy(up_hbm.at[0], wu, w_sem.at[1]),
        pltpu.make_async_copy(down_hbm.at[0], wd, w_sem.at[2]),
    ]
    for load in loads:
        load.start()

    barrier = pltpu.get_barrier_semaphore()
    for other in (right, left, twin):
        pl.semaphore_signal(barrier, inc=1, device_id=other, device_id_type=MESH)

    def upright(flat):
        size = flat.shape[0]
        same = lax.broadcasted_iota(jnp.int32, (size, size), 0) == lax.broadcasted_iota(jnp.int32, (size, size), 1)
        return lax.dot_general(
            flat, same.astype(jnp.float32).astype(jnp.bfloat16), (((0,), (0,)), ((), ())),
            preferred_element_type=jnp.float32,
        )

    factors = upright(scales[...])
    for block in range(width // LANES):
        columns = slice(block * LANES, (block + 1) * LANES)
        scaled = tokens[:, columns].astype(jnp.float32) * factors[:, block:block + 1]
        rows[0, :count, columns] = scaled.astype(jnp.bfloat16)
    line = lax.broadcasted_iota(jnp.int32, (LANES, count), 0)
    dense = jnp.zeros((LANES, count), jnp.float32)
    for route in range(ids.shape[0]):
        dense = dense + jnp.where(ids[route:route + 1, :] == line % experts, weights[route:route + 1, :], 0.0)
    high = dense.astype(jnp.bfloat16).astype(jnp.float32)
    middle = (dense - high).astype(jnp.bfloat16).astype(jnp.float32)
    low = dense - high - middle
    piece = line // experts
    packed = jnp.where(piece == 0, high, jnp.where(piece == 1, middle, jnp.where(piece == 2, low, 0.0)))
    rows[0, :count, width:] = upright(packed.astype(jnp.bfloat16)).astype(jnp.bfloat16)
    sums[0] = jnp.zeros((count, width), jnp.bfloat16)

    def token_copy(step, way, piece, target):
        size = chunk if piece < PIECES - 1 else chunk + LANES
        part = (pl.ds(way * half, half), pl.ds(piece * chunk, size))
        return pltpu.make_async_remote_copy(
            src_ref=rows.at[step, *part], dst_ref=rows.at[step + 1, *part],
            send_sem=tok_send.at[step, way, piece], recv_sem=tok_recv.at[step + 1, way, piece],
            device_id=target, device_id_type=MESH,
        )

    def swap_copy(step):
        return pltpu.make_async_remote_copy(
            src_ref=rows.at[step, pl.ds(0, count)], dst_ref=rows.at[step, pl.ds(count, count)],
            send_sem=swap_send.at[step], recv_sem=swap_recv.at[step],
            device_id=twin, device_id_type=MESH,
        )

    def part_copy(step):
        return pltpu.make_async_remote_copy(
            src_ref=part_out.at[step % 2], dst_ref=part_in.at[step],
            send_sem=part_send.at[step], recv_sem=part_recv.at[step],
            device_id=twin, device_id_type=MESH,
        )

    def sum_copy(step, way, piece, target):
        part = (pl.ds(way * half, half), pl.ds(piece * chunk, chunk))
        return pltpu.make_async_remote_copy(
            src_ref=sums.at[step - 1, *part], dst_ref=sums.at[step, *part],
            send_sem=sum_send.at[step - 1, way, piece], recv_sem=sum_recv.at[step, way, piece],
            device_id=target, device_id_type=MESH,
        )

    def pass_on(step):
        for piece in range(PIECES):
            @pl.when(step > 0)
            def _():
                for way, target in ways:
                    token_copy(step - 1, way, piece, target).wait_recv()

            @pl.when(step < chips - 1)
            def _():
                for way, target in ways:
                    token_copy(step, way, piece, target).start()

        swap_copy(step).start()

    def up_phase(pair):
        def up_tile(tile, carry):
            columns = pl.ds(pl.multiple_of(tile * TILE, TILE), TILE)
            block = rows[pl.ds(2 * pair, 2), :, :width].reshape(4 * count, width)
            gate = jnp.dot(block, wg[:, columns], preferred_element_type=jnp.float32)
            up = jnp.dot(block, wu[:, columns], preferred_element_type=jnp.float32)
            hidden[:, columns] = (gate / (1.0 + jnp.exp(-gate)) * up).astype(jnp.bfloat16)
            return carry

        lax.fori_loop(0, hidden.shape[1] // TILE, up_tile, 0)

    def down_phase(pair):
        lane = lax.broadcasted_iota(jnp.int32, (4 * count, LANES), 1)
        packed = rows[pl.ds(2 * pair, 2), :, width:].reshape(4 * count, LANES).astype(jnp.float32)
        share = jnp.sum(jnp.where(lane % experts == me, packed, 0.0), axis=1, keepdims=True)

        def down_tile(tile, carry):
            columns = pl.ds(pl.multiple_of(tile * TILE, TILE), TILE)
            result = jnp.dot(hidden[...], wd[:, columns], preferred_element_type=jnp.float32) * share
            for turn in range(2):
                at = 2 * turn * count
                own[turn, :, columns] = result[at:at + count]
                part_out[turn, :, columns] = result[at + count:at + 2 * count].astype(jnp.bfloat16)
            return carry

        lax.fori_loop(0, tiles, down_tile, 0)

    pl.semaphore_wait(barrier, 3)
    pass_on(0)
    pass_on(1)
    loads[0].wait()
    loads[1].wait()

    def keep_first():
        part_copy(0).wait_recv()

        def keep_tile(tile, carry):
            columns = pl.ds(pl.multiple_of(tile * TILE, TILE), TILE)
            first[:, columns] = own[0, :, columns] + part_in[0, :, columns].astype(jnp.float32)
            return carry

        lax.fori_loop(0, tiles, keep_tile, 0)

    def send_sums(step):
        part_copy(step).wait_recv()

        for piece in range(PIECES):
            @pl.when(step > 1)
            def _():
                for way, target in ways:
                    sum_copy(step - 1, way, piece, target).wait_recv()

            def add_tile(tile, carry):
                columns = pl.ds(pl.multiple_of(piece * chunk + tile * TILE, TILE), TILE)
                total = own[step % 2, :, columns] + part_in[step, :, columns].astype(jnp.float32)
                total = total + sums[step - 1, :, columns].astype(jnp.float32)
                sums[step - 1, :, columns] = total.astype(jnp.bfloat16)
                return carry

            lax.fori_loop(0, chunk // TILE, add_tile, 0)
            for way, target in ways:
                sum_copy(step, way, piece, target).start()

    def turn(pair, carry):
        swap_copy(2 * pair).wait_recv()
        swap_copy(2 * pair + 1).wait_recv()
        up_phase(pair)

        @pl.when(2 * pair + 2 < chips)
        def _():
            pass_on(2 * pair + 2)

        @pl.when(pair == 0)
        def _():
            loads[2].wait()

        @pl.when(pair > 1)
        def _():
            send_sums(2 * pair - 1)

        @pl.when(pair > 0)
        def _():
            part_copy(2 * pair - 2).wait_send()
            part_copy(2 * pair - 1).wait_send()

        down_phase(pair)
        part_copy(2 * pair).start()
        part_copy(2 * pair + 1).start()

        @pl.when(2 * pair + 3 < chips)
        def _():
            pass_on(2 * pair + 3)

        @pl.when(pair == 0)
        def _():
            send_sums(1)
            keep_first()

        @pl.when(pair > 0)
        def _():
            send_sums(2 * pair)

        return carry

    lax.fori_loop(0, chips // 2, turn, 0)
    send_sums(chips - 1)
    for piece in range(PIECES):
        for way, target in ways:
            sum_copy(chips - 1, way, piece, target).wait_recv()

        def last_tile(tile, carry):
            columns = pl.ds(pl.multiple_of(piece * chunk + tile * TILE, TILE), TILE)
            total = first[:, columns] + sums[chips - 1, :, columns].astype(jnp.float32)
            out[:, columns] = total.astype(jnp.bfloat16)
            return carry

        lax.fori_loop(0, chunk // TILE, last_tile, 0)

    part_copy(chips - 1).wait_send()
    part_copy(chips - 2).wait_send()

    def drain(step, carry):
        for way, target in ways:
            for piece in range(PIECES):
                token_copy(step, way, piece, target).wait_send()
                sum_copy(step + 1, way, piece, target).wait_send()
        return carry

    lax.fori_loop(0, chips - 1, drain, 0)

    def drain_swaps(step, carry):
        swap_copy(step).wait_send()
        return carry

    lax.fori_loop(0, chips, drain_swaps, 0)


def body(tokens, scales, expert_ids, route_weights, w_gate, w_up, w_down):
    chips = lax.axis_size("inner")
    experts = lax.axis_size("outer") * chips
    count, width = tokens.shape
    ff = w_gate.shape[2]
    vmem = pl.BlockSpec(memory_space=pltpu.VMEM)
    hbm = pl.BlockSpec(memory_space=pl.ANY)
    dma = pltpu.SemaphoreType.DMA
    flops = 12 * chips * count * width * ff
    return pl.pallas_call(
        functools.partial(kernel, chips, experts),
        out_shape=jax.ShapeDtypeStruct((count, width), jnp.bfloat16),
        in_specs=[vmem] * 4 + [hbm] * 3,
        out_specs=vmem,
        scratch_shapes=[
            pltpu.VMEM((width, ff), jnp.bfloat16),
            pltpu.VMEM((width, ff), jnp.bfloat16),
            pltpu.VMEM((ff, width), jnp.bfloat16),
            pltpu.VMEM((chips, 2 * count, width + LANES), jnp.bfloat16),
            pltpu.VMEM((4 * count, ff), jnp.bfloat16),
            pltpu.VMEM((2, count, width), jnp.float32),
            pltpu.VMEM((count, width), jnp.float32),
            pltpu.VMEM((2, count, width), jnp.bfloat16),
            pltpu.VMEM((chips, count, width), jnp.bfloat16),
            pltpu.VMEM((chips, count, width), jnp.bfloat16),
            dma((3,)),
            dma((chips, 2, PIECES)), dma((chips, 2, PIECES)),
            dma((chips,)), dma((chips,)),
            dma((chips,)), dma((chips,)),
            dma((chips, 2, PIECES)), dma((chips, 2, PIECES)),
        ],
        cost_estimate=pl.CostEstimate(
            flops=flops, bytes_accessed=6 * width * ff, transcendentals=2 * chips * count * ff
        ),
        compiler_params=pltpu.CompilerParams(
            collective_id=0, has_side_effects=True, vmem_limit_bytes=60 * 1024 * 1024
        ),
    )(tokens, scales.T, expert_ids.T, route_weights.T, w_gate, w_up, w_down)


def solution(mesh):
    rows = P(("parts", "outer", "inner"), None)
    weights = P(("outer", "inner"), None, None)
    return jax.shard_map(
        body,
        mesh=mesh,
        in_specs=(rows, rows, rows, rows, weights, weights, weights),
        out_specs=rows,
        check_vma=False,
    )
```

```python
import functools

import jax
import jax.numpy as jnp
from jax import lax
from jax.experimental import pallas as pl
from jax.experimental.pallas import tpu as pltpu
from jax.sharding import PartitionSpec as P

LANES = 128
TILE = 256
PIECES = 2
MESH = pl.DeviceIdType.MESH


def ring_position(chips, index):
    if chips > 8:
        return index
    z, y = index // 2, index % 2
    return z + y * (chips - 1 - 2 * z)


def ring_index(chips, position):
    if chips > 8:
        return position
    back = position // (chips // 2)
    return (1 - back) * 2 * position + back * (2 * (chips - 1 - position) + 1)


def kernel(
    chips, experts,
    tokens, scales, ids, weights, gate_hbm, up_hbm, down_hbm,
    out,
    wg, wu, wd, rows, hidden, own, first, part_out, part_in, sums,
    w_sem, tok_send, tok_recv, swap_send, swap_recv, part_send, part_recv, sum_send, sum_recv,
):
    core = lax.axis_index("outer")
    index = lax.axis_index("inner")
    me = core * chips + index
    position = ring_position(chips, index)
    right = {"inner": ring_index(chips, (position + 1) % chips)}
    left = {"inner": ring_index(chips, (position + chips - 1) % chips)}
    twin = {"outer": 1 - core}
    count, width = tokens.shape
    half = count // 2
    tiles = width // TILE
    chunk = width // PIECES
    ways = ((0, right), (1, left))

    loads = [
        pltpu.make_async_copy(gate_hbm.at[0], wg, w_sem.at[0]),
        pltpu.make_async_copy(up_hbm.at[0], wu, w_sem.at[1]),
        pltpu.make_async_copy(down_hbm.at[0], wd, w_sem.at[2]),
    ]
    for load in loads:
        load.start()

    barrier = pltpu.get_barrier_semaphore()
    for other in (right, left, twin):
        pl.semaphore_signal(barrier, inc=1, device_id=other, device_id_type=MESH)

    def upright(flat):
        size = flat.shape[0]
        same = lax.broadcasted_iota(jnp.int32, (size, size), 0) == lax.broadcasted_iota(jnp.int32, (size, size), 1)
        return lax.dot_general(
            flat, same.astype(jnp.float32).astype(jnp.bfloat16), (((0,), (0,)), ((), ())),
            preferred_element_type=jnp.float32,
        )

    factors = upright(scales[...])
    for block in range(width // LANES):
        columns = slice(block * LANES, (block + 1) * LANES)
        scaled = tokens[:, columns].astype(jnp.float32) * factors[:, block:block + 1]
        rows[0, :count, columns] = scaled.astype(jnp.bfloat16)
    line = lax.broadcasted_iota(jnp.int32, (LANES, count), 0)
    dense = jnp.zeros((LANES, count), jnp.float32)
    for route in range(ids.shape[0]):
        dense = dense + jnp.where(ids[route:route + 1, :] == line % experts, weights[route:route + 1, :], 0.0)
    high = dense.astype(jnp.bfloat16).astype(jnp.float32)
    middle = (dense - high).astype(jnp.bfloat16).astype(jnp.float32)
    low = dense - high - middle
    piece = line // experts
    packed = jnp.where(piece == 0, high, jnp.where(piece == 1, middle, jnp.where(piece == 2, low, 0.0)))
    rows[0, :count, width:] = upright(packed.astype(jnp.bfloat16)).astype(jnp.bfloat16)
    sums[0] = jnp.zeros((count, width), jnp.bfloat16)

    def token_copy(step, way, piece, target):
        size = chunk if piece < PIECES - 1 else chunk + LANES
        part = (pl.ds(way * half, half), pl.ds(piece * chunk, size))
        return pltpu.make_async_remote_copy(
            src_ref=rows.at[step, *part], dst_ref=rows.at[step + 1, *part],
            send_sem=tok_send.at[step, way, piece], recv_sem=tok_recv.at[step + 1, way, piece],
            device_id=target, device_id_type=MESH,
        )

    def swap_copy(step):
        return pltpu.make_async_remote_copy(
            src_ref=rows.at[step, pl.ds(0, count)], dst_ref=rows.at[step, pl.ds(count, count)],
            send_sem=swap_send.at[step], recv_sem=swap_recv.at[step],
            device_id=twin, device_id_type=MESH,
        )

    def part_copy(step, piece):
        columns = pl.ds(piece * chunk, chunk)
        return pltpu.make_async_remote_copy(
            src_ref=part_out.at[step % 2, :, columns], dst_ref=part_in.at[step, :, columns],
            send_sem=part_send.at[step, piece], recv_sem=part_recv.at[step, piece],
            device_id=twin, device_id_type=MESH,
        )

    def sum_copy(step, way, piece, target):
        part = (pl.ds(way * half, half), pl.ds(piece * chunk, chunk))
        return pltpu.make_async_remote_copy(
            src_ref=sums.at[step - 1, *part], dst_ref=sums.at[step, *part],
            send_sem=sum_send.at[step - 1, way, piece], recv_sem=sum_recv.at[step, way, piece],
            device_id=target, device_id_type=MESH,
        )

    def pass_on(step):
        for piece in range(PIECES):
            @pl.when(step > 0)
            def _():
                for way, target in ways:
                    token_copy(step - 1, way, piece, target).wait_recv()

            @pl.when(step < chips - 1)
            def _():
                for way, target in ways:
                    token_copy(step, way, piece, target).start()

        swap_copy(step).start()

    def up_phase(pair):
        def up_tile(tile, carry):
            columns = pl.ds(pl.multiple_of(tile * TILE, TILE), TILE)
            block = rows[pl.ds(2 * pair, 2), :, :width].reshape(4 * count, width)
            gate = jnp.dot(block, wg[:, columns], preferred_element_type=jnp.float32)
            up = jnp.dot(block, wu[:, columns], preferred_element_type=jnp.float32)
            hidden[:, columns] = (gate / (1.0 + jnp.exp(-gate)) * up).astype(jnp.bfloat16)
            return carry

        lax.fori_loop(0, hidden.shape[1] // TILE, up_tile, 0)

    def down_phase(pair):
        lane = lax.broadcasted_iota(jnp.int32, (4 * count, LANES), 1)
        packed = rows[pl.ds(2 * pair, 2), :, width:].reshape(4 * count, LANES).astype(jnp.float32)
        share = jnp.sum(jnp.where(lane % experts == me, packed, 0.0), axis=1, keepdims=True)

        def down_tile(tile, carry):
            columns = pl.ds(pl.multiple_of(tile * TILE, TILE), TILE)
            result = jnp.dot(hidden[...], wd[:, columns], preferred_element_type=jnp.float32) * share
            for turn in range(2):
                at = 2 * turn * count
                own[turn, :, columns] = result[at:at + count]
                part_out[turn, :, columns] = result[at + count:at + 2 * count].astype(jnp.bfloat16)
            return carry

        for piece in range(PIECES):
            lax.fori_loop(piece * chunk // TILE, (piece + 1) * chunk // TILE, down_tile, 0)
            part_copy(2 * pair, piece).start()
            part_copy(2 * pair + 1, piece).start()
            if piece == 0:
                @pl.when(jnp.logical_and(pair > 0, 2 * pair + 3 < chips))
                def _():
                    pass_on(2 * pair + 3)

    pl.semaphore_wait(barrier, 3)
    pass_on(0)
    pass_on(1)
    loads[0].wait()
    loads[1].wait()

    def keep_first():
        for piece in range(PIECES):
            part_copy(0, piece).wait_recv()

        def keep_tile(tile, carry):
            columns = pl.ds(pl.multiple_of(tile * TILE, TILE), TILE)
            first[:, columns] = own[0, :, columns] + part_in[0, :, columns].astype(jnp.float32)
            return carry

        lax.fori_loop(0, tiles, keep_tile, 0)

    def send_sums(step):
        for piece in range(PIECES):
            part_copy(step, piece).wait_recv()

            @pl.when(step > 1)
            def _():
                for way, target in ways:
                    sum_copy(step - 1, way, piece, target).wait_recv()

            def add_tile(tile, carry):
                columns = pl.ds(pl.multiple_of(piece * chunk + tile * TILE, TILE), TILE)
                total = own[step % 2, :, columns] + part_in[step, :, columns].astype(jnp.float32)
                total = total + sums[step - 1, :, columns].astype(jnp.float32)
                sums[step - 1, :, columns] = total.astype(jnp.bfloat16)
                return carry

            lax.fori_loop(0, chunk // TILE, add_tile, 0)
            for way, target in ways:
                sum_copy(step, way, piece, target).start()

    def turn(pair, carry):
        swap_copy(2 * pair).wait_recv()
        swap_copy(2 * pair + 1).wait_recv()
        up_phase(pair)

        @pl.when(2 * pair + 2 < chips)
        def _():
            pass_on(2 * pair + 2)

        @pl.when(pair == 0)
        def _():
            loads[2].wait()

        @pl.when(pair > 1)
        def _():
            send_sums(2 * pair - 1)

        @pl.when(pair > 0)
        def _():
            for piece in range(PIECES):
                part_copy(2 * pair - 2, piece).wait_send()
                part_copy(2 * pair - 1, piece).wait_send()

        down_phase(pair)
        @pl.when(pair == 0)
        def _():
            pass_on(3)
            send_sums(1)
            keep_first()

        @pl.when(pair > 0)
        def _():
            send_sums(2 * pair)

        return carry

    lax.fori_loop(0, chips // 2, turn, 0)
    send_sums(chips - 1)
    for piece in range(PIECES):
        for way, target in ways:
            sum_copy(chips - 1, way, piece, target).wait_recv()

        def last_tile(tile, carry):
            columns = pl.ds(pl.multiple_of(piece * chunk + tile * TILE, TILE), TILE)
            total = first[:, columns] + sums[chips - 1, :, columns].astype(jnp.float32)
            out[:, columns] = total.astype(jnp.bfloat16)
            return carry

        lax.fori_loop(0, chunk // TILE, last_tile, 0)

    for piece in range(PIECES):
        part_copy(chips - 1, piece).wait_send()
        part_copy(chips - 2, piece).wait_send()

    def drain(step, carry):
        for way, target in ways:
            for piece in range(PIECES):
                token_copy(step, way, piece, target).wait_send()
                sum_copy(step + 1, way, piece, target).wait_send()
        return carry

    lax.fori_loop(0, chips - 1, drain, 0)

    def drain_swaps(step, carry):
        swap_copy(step).wait_send()
        return carry

    lax.fori_loop(0, chips, drain_swaps, 0)


def body(tokens, scales, expert_ids, route_weights, w_gate, w_up, w_down):
    chips = lax.axis_size("inner")
    experts = lax.axis_size("outer") * chips
    count, width = tokens.shape
    ff = w_gate.shape[2]
    vmem = pl.BlockSpec(memory_space=pltpu.VMEM)
    hbm = pl.BlockSpec(memory_space=pl.ANY)
    dma = pltpu.SemaphoreType.DMA
    flops = 12 * chips * count * width * ff
    return pl.pallas_call(
        functools.partial(kernel, chips, experts),
        out_shape=jax.ShapeDtypeStruct((count, width), jnp.bfloat16),
        in_specs=[vmem] * 4 + [hbm] * 3,
        out_specs=vmem,
        scratch_shapes=[
            pltpu.VMEM((width, ff), jnp.bfloat16),
            pltpu.VMEM((width, ff), jnp.bfloat16),
            pltpu.VMEM((ff, width), jnp.bfloat16),
            pltpu.VMEM((chips, 2 * count, width + LANES), jnp.bfloat16),
            pltpu.VMEM((4 * count, ff), jnp.bfloat16),
            pltpu.VMEM((2, count, width), jnp.float32),
            pltpu.VMEM((count, width), jnp.float32),
            pltpu.VMEM((2, count, width), jnp.bfloat16),
            pltpu.VMEM((chips, count, width), jnp.bfloat16),
            pltpu.VMEM((chips, count, width), jnp.bfloat16),
            dma((3,)),
            dma((chips, 2, PIECES)), dma((chips, 2, PIECES)),
            dma((chips,)), dma((chips,)),
            dma((chips, PIECES)), dma((chips, PIECES)),
            dma((chips, 2, PIECES)), dma((chips, 2, PIECES)),
        ],
        cost_estimate=pl.CostEstimate(
            flops=flops, bytes_accessed=6 * width * ff, transcendentals=2 * chips * count * ff
        ),
        compiler_params=pltpu.CompilerParams(
            collective_id=0, has_side_effects=True, vmem_limit_bytes=60 * 1024 * 1024
        ),
    )(tokens, scales.T, expert_ids.T, route_weights.T, w_gate, w_up, w_down)


def solution(mesh):
    rows = P(("parts", "outer", "inner"), None)
    weights = P(("outer", "inner"), None, None)
    return jax.shard_map(
        body,
        mesh=mesh,
        in_specs=(rows, rows, rows, rows, weights, weights, weights),
        out_specs=rows,
        check_vma=False,
    )
```
